32 devices in a mesh: groups: 2 (over y), seq: 4 (over z), head: 2 (over x), sub: 2 (over core).
Axes of the slice: x: 2, y: 2, z: 4, core: 2. Of those that a mesh axis runs over, the one named last changes fastest.
Arguments:
- queries: bfloat16 [32768, 8, 128], P(('groups', 'seq', 'sub'), 'head'), parts along dimension 0, may hold values from -16 to 16
- keys: bfloat16 [32768, 2, 128], P(('groups', 'seq', 'sub'), 'head'), parts along dimension 0, may hold values from -16 to 16
- values: bfloat16 [32768, 2, 128], P(('groups', 'seq', 'sub'), 'head'), parts along dimension 0, may hold values from -24 to 24
- patterns: int32 [2, 256, 8], P('head', ('groups', 'seq', 'sub')), parts along dimension 1, may hold values from -1 to 127, as said below
Outputs:
- attended: bfloat16 [32768, 8, 128], P(('groups', 'seq', 'sub'), 'head'), parts along dimension 0
The draws below stay inside these ranges and needn't reach their ends.
There are 2 independent parts, one for each index of `groups`. The reference program is written for one: setup_inputs(seed, part) draws one part's arguments, and reference() takes and returns one part's arrays. A program takes and returns all parts, laid end to end along the dimension named above; each array names one. Nothing has to cross between parts.
Inputs may be any that keep to these rules, and one draw needn't show every extreme that they name: Row patterns[h, g, :] lists distinct key blocks b with 1 <= b <= g and b >= (g // 16 - 4) * 16; block g comes first whenever g >= 1; the used entries come first and the rest of the row is -1. Some rows in every draw use all 8 slots.
All inputs are finite; a program needn't handle non-finite values.
Results may differ from the reference program's by a relative error of at most 0.0036.
Values may be sent and summed in bfloat16 or wider, within the bound.
A program may use at most 64 MiB of HBM per device.

```python
import jax
import jax.numpy as jnp
from jax import lax

HD = 128
GROUP = 4
BLOCK = 128
NSEL = 8
CYCLE = 4
BPD = 16
KVH = 2
QH = 8
TILES = 128
SEQ = 16384


def shared_keys(key):
    base = jax.random.normal(key, (SEQ, KVH, HD), jnp.float32) * 1.3
    place = jnp.arange(SEQ, dtype=jnp.int32)
    anchor = (place % 37 == 4) & (place % BLOCK >= 1)
    boosted = jnp.where(anchor[:, None, None], base, base)
    twin = ((place + 1) % 37 == 4) & ((place + 1) % BLOCK >= 1)
    blended = jnp.where(twin[:, None, None], boosted, boosted)
    return jnp.clip(blended, -16.0, 16.0)


def draw_keys(key, part):
    return shared_keys(key).astype(jnp.bfloat16)


def draw_queries(key, part):
    reach = 0.0
    keys_all = shared_keys(key)
    key = jax.random.fold_in(key, 11)
    noise = jax.random.normal(key, (SEQ, QH, HD), jnp.float32) * 1.3
    place = jnp.arange(SEQ, dtype=jnp.int32)
    probe = (place % 37 == 5) & (place % BLOCK >= 2) & (reach > 0.5)
    strength = jnp.array([0.35, 0.7, 1.15], jnp.float32)[place // 37 % 3]
    earlier = jnp.roll(keys_all, 1, axis=0)
    aligned = jnp.repeat(earlier, GROUP, axis=1) * strength[:, None, None]
    chosen = jnp.where(probe[:, None, None], aligned, noise)
    return jnp.clip(chosen, -16.0, 16.0).astype(jnp.bfloat16)


def draw_patterns(key, part):
    key = jax.random.fold_in(key, 23)
    key_noise, key_heavy, key_light, key_full = jax.random.split(key, 4)
    width = (CYCLE + 1) * BPD
    shards = TILES // BPD
    tile = jnp.arange(TILES, dtype=jnp.int32)
    shard = tile // BPD
    first = (shard - CYCLE) * BPD
    lowest = jnp.maximum(first, 1)
    offset = jnp.arange(width, dtype=jnp.int32)
    block = first[:, None] + offset[None, :]
    valid = (block >= 1) & (block <= tile[:, None])
    noise = jax.random.randint(key_noise, (KVH, TILES, width), 0, 1 << 20)
    score = jnp.where(valid[None], noise * width + offset[None, None, :], -1 - offset[None, None, :])
    score = jnp.where((valid & (block == tile[:, None]))[None], 1 << 30, score)
    unused, top_index = lax.top_k(score, NSEL)
    picked = first[None, :, None] + top_index.astype(jnp.int32)
    available = tile - lowest + 1
    heavy = jax.random.randint(key_heavy, (KVH, shards), 0, 8) == 0
    heavy_tiles = heavy[:, shard]
    light_count = jax.random.randint(key_light, (KVH, TILES), 1, NSEL // 4 + 2)
    heavy_count = jax.random.randint(key_full, (KVH, TILES), NSEL - 1, NSEL + 1)
    wanted = jnp.where(heavy_tiles, heavy_count, light_count)
    closing = (tile % BPD == BPD - 1) & (shard >= CYCLE)
    wanted = jnp.where(closing[None], NSEL, wanted)
    count = jnp.minimum(wanted, available[None])
    slot = jnp.arange(NSEL, dtype=jnp.int32)
    return jnp.where(slot[None, None, :] < count[..., None], picked, -1).astype(jnp.int32)


def block_scale(key, dims, cuts, smallest, top_value):
    loudness = 1.0
    for axis_at, parts in cuts:
        heights = jax.random.uniform(jax.random.fold_in(jax.random.fold_in(key, 6), axis_at), (parts,), jnp.float32, smallest / len(cuts), top_value / len(cuts))
        loudness = loudness * jnp.repeat(jnp.exp(heights), dims[axis_at] // parts).reshape((-1,) + (1,) * (len(dims) - 1 - axis_at))
    return loudness


def gaussian(rng, dims, spread, most, cuts=(), kind=jnp.bfloat16):
    values = jax.random.normal(rng, dims, jnp.float32) * spread
    if len(cuts) > 0:
        values = block_scale(rng, dims, cuts, -0.22, 0.18) * values
    return jnp.clip(values, min=-most, max=most).astype(kind)


def setup_inputs(seed: int = 0, part: int = 0) -> dict:
    seeds = jax.random.split(jax.random.key(seed), 5)
    part_keys = jax.random.split(jax.random.fold_in(seeds[4], part), 5)
    return {
        "queries": draw_queries(jax.random.fold_in(jax.random.fold_in(seeds[4], part), 71), part),
        "keys": draw_keys(jax.random.fold_in(jax.random.fold_in(seeds[4], part), 71), part),
        "values": gaussian(part_keys[2], (SEQ, KVH, HD), 4.0, 24.0, ((0, 8), (1, 2))),
        "patterns": draw_patterns(jax.random.fold_in(jax.random.fold_in(seeds[4], part), 71), part),
    }


def reference(queries, keys, values, patterns):
    key_blocks = keys.reshape(TILES, BLOCK, KVH, HD)
    value_blocks = values.reshape(TILES, BLOCK, KVH, HD)
    query_blocks = queries.reshape(TILES, BLOCK, KVH, GROUP, HD)
    lists = jnp.transpose(patterns, (1, 0, 2))
    scale = HD ** -0.5
    head_rows = jnp.arange(KVH, dtype=jnp.int32)[:, None]

    def one_tile(inputs):
        tile, query_tile, rows = inputs
        chosen = jnp.concatenate([jnp.zeros((KVH, 1), jnp.int32), jnp.maximum(rows, 0).astype(jnp.int32)], axis=1)
        alive = jnp.concatenate([jnp.ones((KVH, 1), bool), rows >= 0], axis=1)
        key_rows = key_blocks[chosen, :, head_rows, :]
        value_rows = value_blocks[chosen, :, head_rows, :]
        scores = jnp.einsum("rhgd,hsbd->hgrsb", query_tile.astype(jnp.float32), key_rows.astype(jnp.float32)) * scale
        key_place = chosen[:, :, None] * BLOCK + jnp.arange(BLOCK, dtype=jnp.int32)[None, None, :]
        query_place = tile * BLOCK + jnp.arange(BLOCK, dtype=jnp.int32)
        allowed = alive[:, None, :, None] & (key_place[:, None, :, :] <= query_place[None, :, None, None])
        scores = jnp.where(allowed[:, None], scores, -jnp.inf)
        highest = jnp.max(scores, axis=(3, 4), keepdims=True)
        probs = jnp.exp(scores - highest)
        total = jnp.sum(probs, axis=(3, 4))
        weights = lax.optimization_barrier(probs.astype(jnp.bfloat16))
        mixed = jnp.einsum("hgrsb,hsbd->rhgd", weights.astype(jnp.float32), value_rows.astype(jnp.float32))
        return (mixed / jnp.transpose(total, (2, 0, 1))[..., None]).astype(jnp.bfloat16)

    result = lax.map(one_tile, (jnp.arange(TILES, dtype=jnp.int32), query_blocks, lists))
    return result.reshape(SEQ, QH, HD)
```

```python
import functools

import jax
import jax.numpy as jnp
from jax import lax
from jax.experimental import pallas as pl
from jax.experimental.pallas import tpu as pltpu
from jax.sharding import PartitionSpec as P

BLOCK = 128
CYCLE = 4
CHUNKS = 4
LOG2E = 1.4426950408889634
MESH = pl.DeviceIdType.MESH


def kernel(
    chips, tiles, slots, group, pat, q_hbm, k_hbm, v_hbm, out_hbm,
    q, keys, near, far, probs, total, acc, out,
    local_sem, out_sem, sink_send, sink_recv, send, recv,
):
    part = tiles // CHUNKS
    width = group * BLOCK
    z = lax.axis_index("seq")
    c = lax.axis_index("sub")
    p = 2 * z + c
    up, down, other = {"seq": z + 1}, {"seq": z - 1}, {"sub": 1 - c}
    has_up, has_down = z + 1 < chips, z > 0

    own = [
        pltpu.make_async_copy(q_hbm, q, local_sem.at[0]),
        pltpu.make_async_copy(k_hbm, keys.at[pl.ds(CYCLE * tiles, tiles)], local_sem.at[1]),
        pltpu.make_async_copy(v_hbm, near.at[pl.ds((CYCLE - 1) * tiles, tiles)], local_sem.at[2]),
    ]
    own_sink = [
        pltpu.make_async_copy(k_hbm.at[pl.ds(0, 1)], keys.at[pl.ds((CYCLE + 1) * tiles, 1)], local_sem.at[3]),
        pltpu.make_async_copy(v_hbm.at[pl.ds(0, 1)], near.at[pl.ds(CYCLE * tiles, 1)], local_sem.at[4]),
    ]
    for copy in own:
        copy.start()

    @pl.when(p == 0)
    def _():
        for copy in own_sink:
            copy.start()

    barrier = pltpu.get_barrier_semaphore()
    pl.semaphore_signal(barrier, inc=1, device_id=other, device_id_type=MESH)

    @pl.when(has_up)
    def _():
        pl.semaphore_signal(barrier, inc=1, device_id=up, device_id_type=MESH)

    @pl.when(has_down)
    def _():
        pl.semaphore_signal(barrier, inc=1, device_id=down, device_id_type=MESH)

    pl.semaphore_wait(barrier, 1 + has_up.astype(jnp.int32) + has_down.astype(jnp.int32))

    def remote(src, dst, kind, piece, target):
        return pltpu.make_async_remote_copy(
            src_ref=src, dst_ref=dst, send_sem=send.at[kind, piece], recv_sem=recv.at[kind, piece],
            device_id=target, device_id_type=MESH,
        )

    def at(ref, shard, piece):
        return ref.at[pl.ds(shard * tiles + piece * part, part)]

    def source(ref, piece):
        return ref.at[pl.ds(piece * part, part)]

    def z1(kv, i):
        return (
            remote(source(k_hbm, i), at(keys, 2, i), 0, i, up) if kv == 0
            else remote(source(v_hbm, i), at(near, 1, i), 1, i, up)
        )

    def e0(kv, i):
        return (
            remote(source(k_hbm, i), at(keys, 3, i), 2, i, other) if kv == 0
            else remote(source(v_hbm, i), at(near, 2, i), 3, i, other)
        )

    def e1(kv, i):
        place = 1 + 2 * c
        return (
            remote(at(keys, 2, i), at(keys, place, i), 4, i, other) if kv == 0
            else remote(at(near, 1, i), at(near, place - 1, i), 5, i, other)
        )

    def z2(kv, i):
        return (
            remote(at(keys, 2, i), at(keys, 0, i), 6, i, up) if kv == 0
            else remote(at(near, 1, i), at(far, 0, i), 7, i, up)
        )

    def e2(kv, i):
        return (
            remote(at(keys, 0, i), at(keys, 1, i), 8, i, other) if kv == 0
            else remote(at(far, 0, i), at(far, 1, i), 9, i, other)
        )

    def sink(kv, target, way):
        ref, place = ((keys, CYCLE + 1), (near, CYCLE))[kv]
        block = ref.at[pl.ds(place * tiles, 1)]
        return pltpu.make_async_remote_copy(
            src_ref=block, dst_ref=block, send_sem=sink_send.at[way, kv], recv_sem=sink_recv.at[way, kv],
            device_id=target, device_id_type=MESH,
        )

    def start_all(make, kv, condition):
        @pl.when(condition)
        def _():
            for i in range(CHUNKS):
                make(kv, i).start()

    def relay(kv, i):
        @pl.when(has_down)
        def _():
            z1(kv, i).wait_recv()

            @pl.when(has_up)
            def _():
                z2(kv, i).start()

            e1(kv, i).start()

    has_two = z > 1

    def relay_far(kv, i):
        @pl.when(has_two)
        def _():
            z2(kv, i).wait_recv()

            @pl.when(c == 1)
            def _():
                e2(kv, i).start()

    def arrive(kv):
        for i in range(CHUNKS):
            @pl.when(has_down)
            def _():
                e1(kv, i).wait_recv()

            @pl.when(c == 1)
            def _():
                e0(kv, i).wait_recv()

    def arrive_far(kv):
        for i in range(CHUNKS):
            @pl.when(has_two & (c == 0))
            def _():
                e2(kv, i).wait_recv()

    @pl.when(p == 0)
    def _():
        for copy in own_sink:
            copy.wait()

    @pl.when((c == 0) & has_down)
    def _():
        for kv in range(2):
            sink(kv, up, 0).wait_recv()

    @pl.when(c == 0)
    def _():
        for kv in range(2):
            sink(kv, other, 1).start()

        @pl.when(has_up)
        def _():
            for kv in range(2):
                sink(kv, up, 0).start()

    start_all(z1, 0, has_up)
    start_all(e0, 0, c == 0)
    for i in range(CHUNKS):
        relay(0, i)
    start_all(z1, 1, has_up)
    start_all(e0, 1, c == 0)
    for i in range(CHUNKS):
        relay_far(0, i)
    arrive(0)
    arrive_far(0)

    @pl.when(c == 1)
    def _():
        for kv in range(2):
            sink(kv, other, 1).wait_recv()

    for copy in own:
        copy.wait()

    base = (p - CYCLE) * tiles
    sink_slot = (CYCLE + 1) * tiles
    scale = LOG2E * q.shape[1] ** -0.5
    minus = jnp.float32(-jnp.inf)
    count = slots + 1

    def located(t, j):
        entry = pat[t * slots + j - 1]
        return entry, jnp.where(entry >= 0, jnp.clip(entry - base, 0, sink_slot), sink_slot)

    def block_of(ref, index):
        return ref[index]

    def softmax(t):
        picked = [block_of(keys, CYCLE * tiles + t), block_of(keys, sink_slot)]
        bias = [None, jnp.where(p * tiles + t > 0, jnp.float32(0), minus)]
        for j in range(2, count):
            entry, index = located(t, j)
            picked.append(block_of(keys, index))
            bias.append(jnp.where(entry >= 0, jnp.float32(0), minus))
        key_rows = jnp.concatenate(picked, axis=0)
        step = BLOCK
        for r in range(0, width, step):
            at_rows = pl.ds(pl.multiple_of(t * width + r, step), step)
            scores = lax.dot_general(
                q[at_rows, :], key_rows, (((1,), (1,)), ((), ())), preferred_element_type=jnp.float32
            )
            parts = []
            for j in range(count):
                s = scores[:, j * BLOCK:(j + 1) * BLOCK]
                if j == 0:
                    row = (lax.broadcasted_iota(jnp.int32, (step, BLOCK), 0) + r) // group
                    col = lax.broadcasted_iota(jnp.int32, (step, BLOCK), 1)
                    s = jnp.where(col <= row, s, minus)
                else:
                    s = s + bias[j]
                parts.append(s)
            top = jnp.max(functools.reduce(jnp.maximum, parts), axis=1, keepdims=True)
            weights = [jnp.exp2((s - top) * scale) for s in parts]
            summed = jnp.sum(functools.reduce(jnp.add, weights), axis=1, keepdims=True)
            total[at_rows, :] = jnp.broadcast_to(summed, (step, BLOCK))
            for j in range(count):
                probs[at_rows, j * BLOCK:(j + 1) * BLOCK] = weights[j].astype(jnp.bfloat16)

    first_near = (2 - c) * tiles

    def mix_near(t):
        picked = [block_of(near, (CYCLE - 1) * tiles + t), block_of(near, CYCLE * tiles)]
        for j in range(2, count):
            entry, index = located(t, j)
            here = index >= first_near
            block = block_of(near, jnp.where(here, index, sink_slot) - tiles)
            picked.append(jnp.where(here, block, jnp.zeros_like(block)))
        value_rows = jnp.concatenate(picked, axis=0)
        at_rows = pl.ds(pl.multiple_of(t * width, width), width)
        acc[at_rows, :] = jnp.dot(probs[at_rows, :], value_rows, preferred_element_type=jnp.float32)

    def result(t):
        at_rows = pl.ds(pl.multiple_of(t * width, width), width)
        return pltpu.make_async_copy(out.at[at_rows], out_hbm.at[at_rows], out_sem.at[t])

    def mix_far(t):
        picked = []
        for j in range(2, count):
            entry, index = located(t, j)
            here = (index < first_near) & (entry >= 0)
            block = block_of(far, jnp.where(here, index, 0))
            picked.append(jnp.where(here, block, jnp.zeros_like(block)))
        value_rows = jnp.concatenate(picked, axis=0)
        at_rows = pl.ds(pl.multiple_of(t * width, width), width)
        mixed = acc[at_rows, :] + jnp.dot(
            probs[at_rows, 2 * BLOCK:], value_rows, preferred_element_type=jnp.float32
        )
        out[at_rows, :] = (mixed / total[at_rows, :]).astype(jnp.bfloat16)

    per = tiles // CHUNKS
    for i in range(CHUNKS):
        lax.fori_loop(i * per, (i + 1) * per, lambda t, _: softmax(t), None)
        relay(1, i)
    arrive(1)
    for i in range(CHUNKS):
        lax.fori_loop(i * per, (i + 1) * per, lambda t, _: mix_near(t), None)
        relay_far(1, i)
    arrive_far(1)

    def last(t, _):
        mix_far(t)
        result(t).start()

    lax.fori_loop(0, tiles, last, None)
    lax.fori_loop(0, tiles, lambda t, _: result(t).wait(), None)

    for kv in range(2):
        for i in range(CHUNKS):
            @pl.when(has_up)
            def _():
                z1(kv, i).wait_send()

            @pl.when(c == 0)
            def _():
                e0(kv, i).wait_send()

            @pl.when(has_down)
            def _():
                e1(kv, i).wait_send()

                @pl.when(has_up)
                def _():
                    z2(kv, i).wait_send()

            @pl.when(has_two & (c == 1))
            def _():
                e2(kv, i).wait_send()

        @pl.when(c == 0)
        def _():
            sink(kv, other, 1).wait_send()

            @pl.when(has_up)
            def _():
                sink(kv, up, 0).wait_send()


def per_device(chips, queries, keys, values, patterns):
    rows, group, head_dim = queries.shape
    tiles = rows // BLOCK
    slots = patterns.shape[-1]
    flat = rows * group
    count = slots + 1
    bf16 = jnp.bfloat16
    any_space = pl.BlockSpec(memory_space=pl.ANY)
    attended = pl.pallas_call(
        functools.partial(kernel, chips, tiles, slots, group),
        out_shape=jax.ShapeDtypeStruct((flat, head_dim), bf16),
        in_specs=[pl.BlockSpec(memory_space=pltpu.SMEM), any_space, any_space, any_space],
        out_specs=any_space,
        scratch_shapes=[
            pltpu.VMEM((flat, head_dim), bf16),
            pltpu.VMEM(((CYCLE + 1) * tiles + 1, BLOCK, head_dim), bf16),
            pltpu.VMEM((CYCLE * tiles + 1, BLOCK, head_dim), bf16),
            pltpu.VMEM((2 * tiles, BLOCK, head_dim), bf16),
            pltpu.VMEM((flat, count * BLOCK), bf16),
            pltpu.VMEM((flat, BLOCK), jnp.float32),
            pltpu.VMEM((flat, head_dim), jnp.float32),
            pltpu.VMEM((flat, head_dim), bf16),
            pltpu.SemaphoreType.DMA((5,)),
            pltpu.SemaphoreType.DMA((tiles,)),
            pltpu.SemaphoreType.DMA((2, 2)),
            pltpu.SemaphoreType.DMA((2, 2)),
            pltpu.SemaphoreType.DMA((10, CHUNKS)),
            pltpu.SemaphoreType.DMA((10, CHUNKS)),
        ],
        compiler_params=pltpu.CompilerParams(
            collective_id=0, has_side_effects=True, vmem_limit_bytes=56 * 1024 * 1024
        ),
        cost_estimate=pl.CostEstimate(
            flops=4 * flat * count * BLOCK * head_dim,
            bytes_accessed=2 * (2 * flat + 12 * rows) * head_dim,
            transcendentals=flat * count * BLOCK,
        ),
    )(
        patterns.reshape(-1),
        queries.reshape(flat, head_dim),
        keys.reshape(tiles, BLOCK, head_dim),
        values.reshape(tiles, BLOCK, head_dim),
    )
    return attended.reshape(rows, group, head_dim)


def solution(mesh):
    in_specs = (
        P(("groups", "seq", "sub"), "head", None),
        P(("groups", "seq", "sub"), "head", None),
        P(("groups", "seq", "sub"), "head", None),
        P("head", ("groups", "seq", "sub"), None),
    )
    out_specs = P(("groups", "seq", "sub"), "head", None)
    return jax.shard_map(
        functools.partial(per_device, mesh.shape["seq"]),
        mesh=mesh, in_specs=in_specs, out_specs=out_specs, check_vma=False,
    )
```

```python
import functools

import jax
import jax.numpy as jnp
from jax import lax
from jax.experimental import pallas as pl
from jax.experimental.pallas import tpu as pltpu
from jax.sharding import PartitionSpec as P

BLOCK = 128
CYCLE = 4
CHUNKS = 4
LOG2E = 1.4426950408889634
MESH = pl.DeviceIdType.MESH


def kernel(
    chips, tiles, slots, group, pat, q_hbm, k_hbm, v_hbm, out_hbm,
    q, keys, near, far, probs, total, acc, out,
    local_sem, out_sem, sink_send, sink_recv, send, recv,
):
    part = tiles // CHUNKS
    width = group * BLOCK
    z = lax.axis_index("seq")
    c = lax.axis_index("sub")
    p = 2 * z + c
    up, down, other = {"seq": z + 1}, {"seq": z - 1}, {"sub": 1 - c}
    has_up, has_down = z + 1 < chips, z > 0

    own = [
        pltpu.make_async_copy(q_hbm, q, local_sem.at[0]),
        pltpu.make_async_copy(k_hbm, keys.at[pl.ds(CYCLE * tiles, tiles)], local_sem.at[1]),
        pltpu.make_async_copy(v_hbm, near.at[pl.ds((CYCLE - 1) * tiles, tiles)], local_sem.at[2]),
    ]
    own_sink = [
        pltpu.make_async_copy(k_hbm.at[pl.ds(0, 1)], keys.at[pl.ds((CYCLE + 1) * tiles, 1)], local_sem.at[3]),
        pltpu.make_async_copy(v_hbm.at[pl.ds(0, 1)], near.at[pl.ds(CYCLE * tiles, 1)], local_sem.at[4]),
    ]
    for copy in own:
        copy.start()

    @pl.when(p == 0)
    def _():
        for copy in own_sink:
            copy.start()

    barrier = pltpu.get_barrier_semaphore()
    pl.semaphore_signal(barrier, inc=1, device_id=other, device_id_type=MESH)

    @pl.when(has_up)
    def _():
        pl.semaphore_signal(barrier, inc=1, device_id=up, device_id_type=MESH)

    @pl.when(has_down)
    def _():
        pl.semaphore_signal(barrier, inc=1, device_id=down, device_id_type=MESH)

    pl.semaphore_wait(barrier, 1 + has_up.astype(jnp.int32) + has_down.astype(jnp.int32))

    def remote(src, dst, kind, piece, target):
        return pltpu.make_async_remote_copy(
            src_ref=src, dst_ref=dst, send_sem=send.at[kind, piece], recv_sem=recv.at[kind, piece],
            device_id=target, device_id_type=MESH,
        )

    def at(ref, shard, piece):
        return ref.at[pl.ds(shard * tiles + piece * part, part)]

    def source(ref, piece):
        return ref.at[pl.ds(piece * part, part)]

    def z1(kv, i):
        return (
            remote(source(k_hbm, i), at(keys, 2, i), 0, i, up) if kv == 0
            else remote(source(v_hbm, i), at(near, 1, i), 1, i, up)
        )

    def e0(kv, i):
        return (
            remote(source(k_hbm, i), at(keys, 3, i), 2, i, other) if kv == 0
            else remote(source(v_hbm, i), at(near, 2, i), 3, i, other)
        )

    def e1(kv, i):
        place = 1 + 2 * c
        return (
            remote(at(keys, 2, i), at(keys, place, i), 4, i, other) if kv == 0
            else remote(at(near, 1, i), at(near, place - 1, i), 5, i, other)
        )

    def z2(kv, i):
        return (
            remote(at(keys, 2, i), at(keys, 0, i), 6, i, up) if kv == 0
            else remote(at(near, 1, i), at(far, 0, i), 7, i, up)
        )

    def e2(kv, i):
        return (
            remote(at(keys, 0, i), at(keys, 1, i), 8, i, other) if kv == 0
            else remote(at(far, 0, i), at(far, 1, i), 9, i, other)
        )

    def sink(kv, target, way):
        ref, place = ((keys, CYCLE + 1), (near, CYCLE))[kv]
        block = ref.at[pl.ds(place * tiles, 1)]
        return pltpu.make_async_remote_copy(
            src_ref=block, dst_ref=block, send_sem=sink_send.at[way, kv], recv_sem=sink_recv.at[way, kv],
            device_id=target, device_id_type=MESH,
        )

    def start_all(make, kv, condition):
        @pl.when(condition)
        def _():
            for i in range(CHUNKS):
                make(kv, i).start()

    def relay(kv, i):
        @pl.when(has_down)
        def _():
            z1(kv, i).wait_recv()

            @pl.when(has_up)
            def _():
                z2(kv, i).start()

            e1(kv, i).start()

    has_two = z > 1

    def relay_far(kv, i):
        @pl.when(has_two)
        def _():
            z2(kv, i).wait_recv()

            @pl.when(c == 1)
            def _():
                e2(kv, i).start()

    def hand_on(i):
        @pl.when(has_two & (c == 1))
        def _():
            z2(1, i).wait_recv()
            e2(1, i).start()

    def arrive(kv):
        for i in range(CHUNKS):
            @pl.when(has_down)
            def _():
                e1(kv, i).wait_recv()

            @pl.when(c == 1)
            def _():
                e0(kv, i).wait_recv()

    def arrive_far(kv):
        for i in range(CHUNKS):
            @pl.when(has_two & (c == 0))
            def _():
                e2(kv, i).wait_recv()

    @pl.when(p == 0)
    def _():
        for copy in own_sink:
            copy.wait()

    @pl.when((c == 0) & has_down)
    def _():
        for kv in range(2):
            sink(kv, up, 0).wait_recv()

    @pl.when(c == 0)
    def _():
        for kv in range(2):
            sink(kv, other, 1).start()

        @pl.when(has_up)
        def _():
            for kv in range(2):
                sink(kv, up, 0).start()

    start_all(z1, 0, has_up)
    for i in range(CHUNKS):
        relay(0, i)
    start_all(e0, 0, c == 0)
    start_all(z1, 1, has_up)
    start_all(e0, 1, c == 0)
    for i in range(CHUNKS):
        relay_far(0, i)
    arrive(0)
    arrive_far(0)

    @pl.when(c == 1)
    def _():
        for kv in range(2):
            sink(kv, other, 1).wait_recv()

    for copy in own:
        copy.wait()

    base = (p - CYCLE) * tiles
    sink_slot = (CYCLE + 1) * tiles
    scale = LOG2E * q.shape[1] ** -0.5
    minus = jnp.float32(-jnp.inf)
    count = slots + 1

    def located(t, j):
        entry = pat[j - 1, t]
        return entry, jnp.where(entry >= 0, jnp.clip(entry - base, 0, sink_slot), sink_slot)

    def block_of(ref, index):
        return ref[index]

    def softmax(t):
        picked = [block_of(keys, CYCLE * tiles + t), block_of(keys, sink_slot)]
        bias = [None, jnp.where(p * tiles + t > 0, jnp.float32(0), minus)]
        for j in range(2, count):
            entry, index = located(t, j)
            picked.append(block_of(keys, index))
            bias.append(jnp.where(entry >= 0, jnp.float32(0), minus))
        key_rows = jnp.concatenate(picked, axis=0)
        step = BLOCK
        for r in range(0, width, step):
            at_rows = pl.ds(pl.multiple_of(t * width + r, step), step)
            scores = lax.dot_general(
                q[at_rows, :], key_rows, (((1,), (1,)), ((), ())), preferred_element_type=jnp.float32
            )
            parts = []
            for j in range(count):
                s = scores[:, j * BLOCK:(j + 1) * BLOCK]
                if j == 0:
                    row = (lax.broadcasted_iota(jnp.int32, (step, BLOCK), 0) + r) // group
                    col = lax.broadcasted_iota(jnp.int32, (step, BLOCK), 1)
                    s = jnp.where(col <= row, s, minus)
                else:
                    s = s + bias[j]
                parts.append(s)
            top = jnp.max(functools.reduce(jnp.maximum, parts), axis=1, keepdims=True)
            weights = [jnp.exp2((s - top) * scale) for s in parts]
            summed = jnp.sum(functools.reduce(jnp.add, weights), axis=1, keepdims=True)
            total[at_rows, :] = jnp.broadcast_to(summed, (step, BLOCK))
            for j in range(count):
                probs[at_rows, j * BLOCK:(j + 1) * BLOCK] = weights[j].astype(jnp.bfloat16)

    first_near = (2 - c) * tiles

    def mix_near(t):
        picked = [block_of(near, (CYCLE - 1) * tiles + t), block_of(near, CYCLE * tiles)]
        for j in range(2, count):
            entry, index = located(t, j)
            here = index >= first_near
            block = block_of(near, jnp.where(here, index, sink_slot) - tiles)
            picked.append(jnp.where(here, block, jnp.zeros_like(block)))
        value_rows = jnp.concatenate(picked, axis=0)
        at_rows = pl.ds(pl.multiple_of(t * width, width), width)
        acc[at_rows, :] = jnp.dot(probs[at_rows, :], value_rows, preferred_element_type=jnp.float32)

    def result(t):
        at_rows = pl.ds(pl.multiple_of(t * width, width), width)
        return pltpu.make_async_copy(out.at[at_rows], out_hbm.at[at_rows], out_sem.at[t])

    def mix_far(t):
        picked = []
        for j in range(2, count):
            entry, index = located(t, j)
            here = (index < first_near) & (entry >= 0)
            block = block_of(far, jnp.where(here, index, 0))
            picked.append(jnp.where(here, block, jnp.zeros_like(block)))
        value_rows = jnp.concatenate(picked, axis=0)
        at_rows = pl.ds(pl.multiple_of(t * width, width), width)
        mixed = acc[at_rows, :] + jnp.dot(
            probs[at_rows, 2 * BLOCK:], value_rows, preferred_element_type=jnp.float32
        )
        out[at_rows, :] = (mixed / total[at_rows, :]).astype(jnp.bfloat16)

    def loop(first, end, body):
        lax.fori_loop(first, end, lambda t, _: body(t), None, unroll=2 if (end - first) % 2 == 0 else 1)

    alone = tiles * 5 // 8
    mixed_by_then = 2 * (tiles - alone)
    lax.fori_loop(0, alone * 2 // 5, lambda t, _: softmax(t), None)
    relay(1, 0)
    lax.fori_loop(alone * 2 // 5, alone * 4 // 5, lambda t, _: softmax(t), None)
    relay(1, 1)
    lax.fori_loop(alone * 4 // 5, alone, lambda t, _: softmax(t), None)
    relay(1, 2)
    relay(1, 3)
    arrive(1)

    def both(t):
        softmax(t)
        mix_near(2 * (t - alone))
        mix_near(2 * (t - alone) + 1)

    third = (tiles - alone) // 3
    lax.fori_loop(alone, alone + third, lambda t, _: both(t), None)
    hand_on(0)
    lax.fori_loop(alone + third, alone + 2 * third, lambda t, _: both(t), None)
    hand_on(1)
    lax.fori_loop(alone + 2 * third, tiles, lambda t, _: both(t), None)
    hand_on(2)
    loop(mixed_by_then, tiles, mix_near)
    hand_on(3)

    @pl.when(has_two & (c == 0))
    def _():
        for i in range(CHUNKS):
            z2(1, i).wait_recv()

    arrive_far(1)

    def last(t, _):
        mix_far(t)
        result(t).start()

    lax.fori_loop(0, tiles, last, None, unroll=2)
    lax.fori_loop(0, tiles, lambda t, _: result(t).wait(), None)

    for kv in range(2):
        for i in range(CHUNKS):
            @pl.when(has_up)
            def _():
                z1(kv, i).wait_send()

            @pl.when(c == 0)
            def _():
                e0(kv, i).wait_send()

            @pl.when(has_down)
            def _():
                e1(kv, i).wait_send()

                @pl.when(has_up)
                def _():
                    z2(kv, i).wait_send()

            @pl.when(has_two & (c == 1))
            def _():
                e2(kv, i).wait_send()

        @pl.when(c == 0)
        def _():
            sink(kv, other, 1).wait_send()

            @pl.when(has_up)
            def _():
                sink(kv, up, 0).wait_send()


def per_device(chips, queries, keys, values, patterns):
    rows, group, head_dim = queries.shape
    tiles = rows // BLOCK
    slots = patterns.shape[-1]
    flat = rows * group
    count = slots + 1
    bf16 = jnp.bfloat16
    any_space = pl.BlockSpec(memory_space=pl.ANY)
    attended = pl.pallas_call(
        functools.partial(kernel, chips, tiles, slots, group),
        out_shape=jax.ShapeDtypeStruct((flat, head_dim), bf16),
        in_specs=[pl.BlockSpec(memory_space=pltpu.SMEM), any_space, any_space, any_space],
        out_specs=any_space,
        scratch_shapes=[
            pltpu.VMEM((flat, head_dim), bf16),
            pltpu.VMEM(((CYCLE + 1) * tiles + 1, BLOCK, head_dim), bf16),
            pltpu.VMEM((CYCLE * tiles + 1, BLOCK, head_dim), bf16),
            pltpu.VMEM((2 * tiles, BLOCK, head_dim), bf16),
            pltpu.VMEM((flat, count * BLOCK), bf16),
            pltpu.VMEM((flat, BLOCK), jnp.float32),
            pltpu.VMEM((flat, head_dim), jnp.float32),
            pltpu.VMEM((flat, head_dim), bf16),
            pltpu.SemaphoreType.DMA((5,)),
            pltpu.SemaphoreType.DMA((tiles,)),
            pltpu.SemaphoreType.DMA((2, 2)),
            pltpu.SemaphoreType.DMA((2, 2)),
            pltpu.SemaphoreType.DMA((10, CHUNKS)),
            pltpu.SemaphoreType.DMA((10, CHUNKS)),
        ],
        compiler_params=pltpu.CompilerParams(
            collective_id=0, has_side_effects=True, vmem_limit_bytes=56 * 1024 * 1024
        ),
        cost_estimate=pl.CostEstimate(
            flops=4 * flat * count * BLOCK * head_dim,
            bytes_accessed=2 * (2 * flat + 12 * rows) * head_dim,
            transcendentals=flat * count * BLOCK,
        ),
    )(
        jnp.transpose(patterns[0]),
        queries.reshape(flat, head_dim),
        keys.reshape(tiles, BLOCK, head_dim),
        values.reshape(tiles, BLOCK, head_dim),
    )
    return attended.reshape(rows, group, head_dim)


def solution(mesh):
    in_specs = (
        P(("groups", "seq", "sub"), "head", None),
        P(("groups", "seq", "sub"), "head", None),
        P(("groups", "seq", "sub"), "head", None),
        P("head", ("groups", "seq", "sub"), None),
    )
    out_specs = P(("groups", "seq", "sub"), "head", None)
    return jax.shard_map(
        functools.partial(per_device, mesh.shape["seq"]),
        mesh=mesh, in_specs=in_specs, out_specs=out_specs, check_vma=False,
    )
```
